32 devices in a mesh: grp: 2 (over x), tm: 16 (over z, y, core).
Axes of the slice: x: 2, y: 2, z: 4, core: 2. Of those that a mesh axis runs over, the one named last changes fastest.
Arguments:
- queries: bfloat16 [24576, 128], P(('grp', 'tm')), parts along dimension 0, may hold values from -6 to 6
- key_codes: bfloat16 [24576, 128], P(('grp', 'tm')), parts along dimension 0, may hold values from -6 to 6
- value_codes: bfloat16 [24576, 128], P(('grp', 'tm')), parts along dimension 0, may hold values from -6 to 6
- key_scales: float32 [192], P(('grp', 'tm')), parts along dimension 0, may hold values from 0.6 to 1.6
- value_scales: float32 [192], P(('grp', 'tm')), parts along dimension 0, may hold values from 0.3 to 3
- scale_slot: int32 [32, 6], P(('grp', 'tm')), parts along dimension 0, may hold values from 0 to 5, each once within a row
- grad_out: bfloat16 [24576, 128], P(('grp', 'tm')), parts along dimension 0, may hold values from -384 to 384
Outputs:
- query_grad: bfloat16 [24576, 128], P(('grp', 'tm')), parts along dimension 0
- key_grad: bfloat16 [24576, 128], P(('grp', 'tm')), parts along dimension 0
- value_grad: bfloat16 [24576, 128], P(('grp', 'tm')), parts along dimension 0
The draws below stay inside these ranges and needn't reach their ends.
There are 2 independent parts, one for each index of `grp`. The reference program is written for one: setup_inputs(seed, part) draws one part's arguments, and reference() takes and returns one part's arrays. A program takes and returns all parts, laid end to end along the dimension named above; each array names one. Nothing has to cross between parts.
Inputs may be any that keep to these rules, and one draw needn't show every extreme that they name: Row s of scale_slot names every number 0 to 5 once.
All inputs are finite; a program needn't handle non-finite values.
Results may differ from the reference program's by a relative error of at most 0.0019.
The reference program's roundings to bfloat16 on the way count: a program that leaves them out, or rounds other values in their place, can miss the bound.
Values may be sent and summed in bfloat16 or wider, within the bound.
No kernel may reach another device: no remote copies, remote signals or barrier semaphores. Data moves between devices by JAX's collectives and lax.ppermute only.
A program may use at most 64 MiB of HBM per device.

```python
import math
import jax
import jax.numpy as jnp
from jax import lax

HEAD_DIM = 128
TILE_TOKENS = 256
ROW_TILES = 4
QUANT_BLOCK = 128
FRAME_TILES = 4
TOK_DEV = 768
SLABS = 16
TOKENS = 12288
BLOCKS_DEV = 6
BLOCKS = 96


def draw_queries(key, part):
    own_key = jax.random.fold_in(key, 17)
    result = jax.random.truncated_normal(own_key, -6.0, 6.0, (TOKENS, HEAD_DIM), jnp.float32)
    return result.astype(jnp.bfloat16)


def draw_key_codes(key, part):
    own_key = jax.random.fold_in(key, 23)
    result = jax.random.truncated_normal(own_key, -6.0, 6.0, (TOKENS, HEAD_DIM), jnp.float32)
    return result.astype(jnp.bfloat16)


def levels(rng, shape, split, low, high):
    factor_of = 1.0
    for dim, parts in split:
        steps = jax.random.uniform(jax.random.fold_in(jax.random.fold_in(rng, 6), dim), (parts,), jnp.float32, low / len(split), high / len(split))
        factor_of = factor_of * jnp.repeat(jnp.exp(steps), shape[dim] // parts).reshape((-1,) + (1,) * (len(shape) - 1 - dim))
    return factor_of


def bell_draw(rng, dims, scale, limit, pieces=(), kind=jnp.bfloat16):
    loudness = levels(rng, dims, pieces, -0.22, 0.18) if pieces else 1.0
    values = jax.random.normal(rng, dims, jnp.float32) * scale * loudness
    return jnp.minimum(jnp.maximum(values, -limit), limit).astype(kind)


def setup_inputs(seed: int = 0, part: int = 0) -> dict:
    streams_of = jax.random.split(jax.random.key(seed), 8)
    own_keys = jax.random.split(jax.random.fold_in(streams_of[7], part), 8)
    queries = draw_queries(jax.random.fold_in(jax.random.fold_in(streams_of[7], part), 71), part)
    key_codes = draw_key_codes(jax.random.fold_in(jax.random.fold_in(streams_of[7], part), 71), part)
    value_codes = bell_draw(own_keys[2], (TOKENS, HEAD_DIM), 1.0, 6.0, ((0, 16),))
    key_scales = jnp.clip(jnp.exp(math.log(1.6) - 0.98082923 * jax.random.uniform(own_keys[3], (BLOCKS,), jnp.float32) ** levels(own_keys[3], (BLOCKS,), ((0, 16),), -0.2, 0.2)), 0.6, 1.6)
    value_scales = jnp.clip(jnp.exp(math.log(3.0) - 2.3025851 * jax.random.uniform(own_keys[4], (BLOCKS,), jnp.float32) ** levels(own_keys[4], (BLOCKS,), ((0, 16),), -0.2, 0.2)), 0.3, 3.0)
    scale_slot = jax.vmap(lambda own: jax.random.permutation(own, BLOCKS_DEV))(jax.random.split(own_keys[5], SLABS)).reshape((SLABS, BLOCKS_DEV)).astype(jnp.int32)
    grad_out = bell_draw(own_keys[6], (TOKENS, HEAD_DIM), 64.0, 384.0, ((0, 16),))
    return dict(queries=queries, key_codes=key_codes, value_codes=value_codes, key_scales=key_scales, value_scales=value_scales, scale_slot=scale_slot, grad_out=grad_out)


big_negative = -1.0e30
offsets_list = [(frame_step, row_step) for frame_step in (-1, 0, 1) for row_step in (-1, 0, 1)]


def dequantize(code_array, scales, scale_slot):
    slab_base = jnp.arange(SLABS, dtype=jnp.int32)[:, None] * BLOCKS_DEV
    scale_rows = (slab_base + scale_slot).reshape(-1)
    picked = scales[scale_rows]
    blocked = code_array.astype(jnp.float32).reshape(BLOCKS, QUANT_BLOCK, HEAD_DIM)
    return (blocked * picked[:, None, None]).astype(jnp.bfloat16).reshape(TOKENS, HEAD_DIM)


def reference(queries, key_codes, value_codes, key_scales, value_scales, scale_slot, grad_out):
    inverse = HEAD_DIM ** -0.5
    keys_all = dequantize(key_codes, key_scales, scale_slot)
    values_all = dequantize(value_codes, value_scales, scale_slot)

    def padded(array):
        tail_shape = array.shape[1:]
        shaped = array.reshape((FRAME_TILES, ROW_TILES, TOK_DEV) + tail_shape)
        widths = ((1, 1), (1, 1), (0, 0)) + tuple((0, 0) for extent in tail_shape)
        return jnp.pad(shaped, widths)

    zero_index = jnp.zeros((), jnp.int32)

    def take(array_pad, frame_idx, row_idx):
        starts = (frame_idx + 1, row_idx + 1) + tuple(zero_index for extent in array_pad.shape[2:])
        sizes_tuple = (1, 1) + array_pad.shape[2:]
        return lax.dynamic_slice(array_pad, starts, sizes_tuple)[0, 0]

    def inside(frame_idx, row_idx):
        return (frame_idx >= 0) & (frame_idx < FRAME_TILES) & (row_idx >= 0) & (row_idx < ROW_TILES)

    tile_of = jnp.arange(TOK_DEV, dtype=jnp.int32) // TILE_TOKENS
    near_cols = jnp.abs(tile_of[:, None] - tile_of[None, :]) <= 1
    query_pad = padded(queries)
    key_pad = padded(keys_all)
    value_pad = padded(values_all)
    grad_pad = padded(grad_out)

    def forward_slab(slab_id):
        frame_idx = slab_id // ROW_TILES
        row_idx = slab_id % ROW_TILES
        query_block = take(query_pad, frame_idx, row_idx)
        grad_block = take(grad_pad, frame_idx, row_idx)
        score_list, prob_grads, allowed_list, key_list = [], [], [], []
        for frame_step, row_step in offsets_list:
            other_frame = frame_idx + frame_step
            other_row = row_idx + row_step
            key_block = take(key_pad, other_frame, other_row)
            value_block = take(value_pad, other_frame, other_row)
            allowed = near_cols & inside(other_frame, other_row)
            scores = jnp.dot(query_block, key_block.T, preferred_element_type=jnp.float32) * inverse
            score_list.append(jnp.where(allowed, scores, big_negative))
            prob_grads.append(jnp.dot(grad_block, value_block.T, preferred_element_type=jnp.float32))
            allowed_list.append(allowed)
            key_list.append(key_block)
        scores = jnp.concatenate(score_list, axis=1)
        allowed_all = jnp.concatenate(allowed_list, axis=1)
        grad_prob = jnp.concatenate(prob_grads, axis=1)
        row_top = jnp.max(scores, axis=1, keepdims=True)
        summed = jnp.sum(jnp.where(allowed_all, jnp.exp(scores - row_top), 0.0), axis=1)
        log_total = row_top[:, 0] + jnp.log(summed)
        attn_prob = jnp.where(allowed_all, jnp.exp(scores - log_total[:, None]), 0.0)
        row_delta = jnp.sum(attn_prob * grad_prob, axis=1)
        dscore = (attn_prob * (grad_prob - row_delta[:, None])).astype(jnp.bfloat16)
        key_window = jnp.concatenate(key_list, axis=0)
        query_grad = (jnp.dot(dscore, key_window, preferred_element_type=jnp.float32) * inverse).astype(jnp.bfloat16)
        return query_grad, log_total, row_delta

    slab_ids = jnp.arange(SLABS, dtype=jnp.int32)
    query_grads, log_totals, row_deltas = lax.map(forward_slab, slab_ids)
    total_pad = padded(log_totals.reshape(TOKENS))
    delta_pad = padded(row_deltas.reshape(TOKENS))

    def backward_slab(slab_id):
        frame_idx = slab_id // ROW_TILES
        row_idx = slab_id % ROW_TILES
        key_block = take(key_pad, frame_idx, row_idx)
        value_block = take(value_pad, frame_idx, row_idx)
        key_sum = jnp.zeros((TOK_DEV, HEAD_DIM), jnp.float32)
        value_sum = jnp.zeros((TOK_DEV, HEAD_DIM), jnp.float32)
        for frame_step, row_step in offsets_list:
            other_frame = frame_idx + frame_step
            other_row = row_idx + row_step
            query_block = take(query_pad, other_frame, other_row)
            grad_block = take(grad_pad, other_frame, other_row)
            total_block = take(total_pad, other_frame, other_row)
            delta_block = take(delta_pad, other_frame, other_row)
            allowed = near_cols & inside(other_frame, other_row)
            scores = jnp.dot(query_block, key_block.T, preferred_element_type=jnp.float32) * inverse
            attn_prob = jnp.where(allowed, jnp.exp(scores - total_block[:, None]), 0.0)
            grad_prob = jnp.dot(grad_block, value_block.T, preferred_element_type=jnp.float32)
            dscore = (attn_prob * (grad_prob - delta_block[:, None])).astype(jnp.bfloat16)
            key_part = jnp.dot(dscore.T, query_block, preferred_element_type=jnp.float32) * inverse
            value_part = jnp.dot(attn_prob.astype(jnp.bfloat16).T, grad_block, preferred_element_type=jnp.float32)
            key_sum = key_sum + lax.optimization_barrier(key_part.astype(jnp.bfloat16)).astype(jnp.float32)
            value_sum = value_sum + lax.optimization_barrier(value_part.astype(jnp.bfloat16)).astype(jnp.float32)
        return key_sum.astype(jnp.bfloat16), value_sum.astype(jnp.bfloat16)

    key_grads, value_grads = lax.map(backward_slab, slab_ids)
    return (query_grads.reshape(TOKENS, HEAD_DIM), key_grads.reshape(TOKENS, HEAD_DIM), value_grads.reshape(TOKENS, HEAD_DIM))
```

```python
import functools
import math

import jax
import jax.numpy as jnp
from jax import lax
from jax.experimental import pallas as pl
from jax.experimental.pallas import tpu as pltpu
from jax.sharding import PartitionSpec as P

HEAD_DIM = 128
TILE_TOKENS = 256
ROW_TILES = 4
CHIP_ROWS = 2

SCALE = HEAD_DIM ** (-0.5)
SCALE2 = SCALE * math.log2(math.e)
BIG_NEGATIVE = -1e30
VMEM_LIMIT = 48 * 2**20

F32 = jnp.float32
BF16 = jnp.bfloat16
NT = (((1,), (1,)), ((), ()))
TN = (((0,), (0,)), ((), ()))
NN = (((1,), (0,)), ((), ()))


def dot(left, right, dims):
    return lax.dot_general(left, right, dims, preferred_element_type=F32)


def near(tile, tokens):
    return max(0, tile - 1) * TILE_TOKENS, min(tokens, (tile + 2) * TILE_TOKENS)


def whole(*shape):
    return pl.BlockSpec(shape, lambda j, valid: (0,) * len(shape))


def stacked(*shape):
    return pl.BlockSpec((1,) + shape, lambda j, valid: (j,) + (0,) * len(shape))


def params():
    return pltpu.CompilerParams(vmem_limit_bytes=VMEM_LIMIT)


def prepare_kernel(key_scales, value_scales, slots, queries, key_codes, value_codes, grad_out, kv, qg):
    blocks = slots.shape[1]
    size = queries.shape[0] // blocks
    for block in range(blocks):
        rows = slice(block * size, (block + 1) * size)
        slot = slots[0, block]
        kv[0, rows] = (key_codes[rows].astype(F32) * key_scales[slot]).astype(BF16)
        kv[1, rows] = (value_codes[rows].astype(F32) * value_scales[slot]).astype(BF16)
    qg[0] = queries[...]
    qg[1] = grad_out[...]


def prepare(queries, key_codes, value_codes, key_scales, value_scales, slots, grad_out):
    smem = pl.BlockSpec(memory_space=pltpu.SMEM)
    vmem = pl.BlockSpec(memory_space=pltpu.VMEM)
    pair = jax.ShapeDtypeStruct((2,) + queries.shape, BF16)
    return pl.pallas_call(
        prepare_kernel,
        in_specs=[smem, smem, smem, vmem, vmem, vmem, vmem],
        out_specs=[vmem, vmem],
        out_shape=[pair, pair],
        compiler_params=params(),
        name="prepare",
    )(key_scales, value_scales, slots, queries, key_codes, value_codes, grad_out)


def stats_kernel(finish, valid, qg, kv, start, out, *final):
    step = pl.program_id(0)
    tokens = qg.shape[1]

    @pl.when(step == 0)
    def _():
        out[...] = start[...]

    @pl.when(valid[step] > 0)
    def _():
        for tile in range(tokens // TILE_TOKENS):
            cols = slice(tile * TILE_TOKENS, (tile + 1) * TILE_TOKENS)
            low, high = near(tile, tokens)
            shape = ((high - low) // 8, 8, TILE_TOKENS)
            scores = (dot(kv[0, 0, low:high], qg[0, cols], NT) * SCALE2).reshape(shape)
            grad_prob = dot(kv[0, 1, low:high], qg[1, cols], NT).reshape(shape)
            top = out[0, :, cols]
            new_top = jnp.maximum(top, jnp.max(scores, axis=0))
            unscaled = jnp.exp2(scores - new_top[None])
            rescale = jnp.exp2(top - new_top)
            out[0, :, cols] = new_top
            out[1, :, cols] = out[1, :, cols] * rescale + jnp.sum(unscaled, axis=0)
            out[2, :, cols] = out[2, :, cols] * rescale + jnp.sum(unscaled * grad_prob, axis=0)

    if finish:

        @pl.when(step == pl.num_programs(0) - 1)
        def _():
            top = out[0]
            row_top = jnp.max(top, axis=0, keepdims=True)
            rescale = jnp.exp2(top - row_top)
            total = jnp.sum(out[1] * rescale, axis=0, keepdims=True)
            weighted = jnp.sum(out[2] * rescale, axis=0, keepdims=True)
            final[0][0:1] = row_top + jnp.log2(total)
            final[0][1:2] = weighted / total


def stats(valid, qg, kv, start, finish):
    count, _, tokens, dim = kv.shape
    shapes = [jax.ShapeDtypeStruct((3, 8, tokens), F32)]
    specs = [whole(3, 8, tokens)]
    if finish:
        shapes.append(jax.ShapeDtypeStruct((2, tokens), F32))
        specs.append(whole(2, tokens))
    return pl.pallas_call(
        functools.partial(stats_kernel, finish),
        grid_spec=pltpu.PrefetchScalarGridSpec(
            num_scalar_prefetch=1,
            grid=(count,),
            in_specs=[whole(2, tokens, dim), stacked(2, tokens, dim), whole(3, 8, tokens)],
            out_specs=specs,
        ),
        out_shape=shapes,
        compiler_params=params(),
        name="row_stats",
    )(valid, qg, kv, start)


def query_kernel(valid, qg, kv, rows, out, total):
    step = pl.program_id(0)
    tokens = qg.shape[1]

    @pl.when(step == 0)
    def _():
        total[...] = jnp.zeros_like(total)

    @pl.when(valid[step] > 0)
    def _():
        for tile in range(tokens // TILE_TOKENS):
            cols = slice(tile * TILE_TOKENS, (tile + 1) * TILE_TOKENS)
            low, high = near(tile, tokens)
            keys = kv[0, 0, low:high]
            scores = dot(keys, qg[0, cols], NT)
            attn_prob = jnp.exp2(scores * SCALE2 - rows[0:1, cols])
            grad_prob = dot(kv[0, 1, low:high], qg[1, cols], NT)
            dscore = (attn_prob * (grad_prob - rows[1:2, cols])).astype(BF16)
            total[:, cols] += dot(keys, dscore, TN)

    @pl.when(step == pl.num_programs(0) - 1)
    def _():
        out[...] = (total[...] * SCALE).T.astype(BF16)


def query_side(valid, qg, kv, rows):
    count, _, tokens, dim = kv.shape
    return pl.pallas_call(
        query_kernel,
        grid_spec=pltpu.PrefetchScalarGridSpec(
            num_scalar_prefetch=1,
            grid=(count,),
            in_specs=[whole(2, tokens, dim), stacked(2, tokens, dim), whole(2, tokens)],
            out_specs=whole(tokens, dim),
            scratch_shapes=[pltpu.VMEM((dim, tokens), F32)],
        ),
        out_shape=jax.ShapeDtypeStruct((tokens, dim), BF16),
        compiler_params=params(),
        name="query_side",
    )(valid, qg, kv, rows)


def key_kernel(valid, kv, qg, rows, key_out, value_out, total):
    step = pl.program_id(0)
    tokens = kv.shape[1]

    @pl.when(step == 0)
    def _():
        total[...] = jnp.zeros_like(total)

    @pl.when(valid[step] > 0)
    def _():
        for tile in range(tokens // TILE_TOKENS):
            cols = slice(tile * TILE_TOKENS, (tile + 1) * TILE_TOKENS)
            low, high = near(tile, tokens)
            queries = qg[0, 0, low:high]
            grads = qg[0, 1, low:high]
            scores = dot(kv[0, cols], queries, NT)
            attn_prob = jnp.exp2(scores * SCALE2 - rows[0, 0:1, low:high])
            grad_prob = dot(kv[1, cols], grads, NT)
            dscore = (attn_prob * (grad_prob - rows[0, 1:2, low:high])).astype(BF16)
            key_part = (dot(dscore, queries, NN) * SCALE).astype(BF16)
            value_part = dot(attn_prob.astype(BF16), grads, NN).astype(BF16)
            total[0, cols] += key_part.astype(F32)
            total[1, cols] += value_part.astype(F32)

    @pl.when(step == pl.num_programs(0) - 1)
    def _():
        key_out[...] = total[0].astype(BF16)
        value_out[...] = total[1].astype(BF16)


def key_side(valid, kv, qg, rows):
    count, _, tokens, dim = qg.shape
    return pl.pallas_call(
        key_kernel,
        grid_spec=pltpu.PrefetchScalarGridSpec(
            num_scalar_prefetch=1,
            grid=(count,),
            in_specs=[whole(2, tokens, dim), stacked(2, tokens, dim), stacked(2, tokens)],
            out_specs=[whole(tokens, dim), whole(tokens, dim)],
            scratch_shapes=[pltpu.VMEM((2, tokens, dim), F32)],
        ),
        out_shape=[jax.ShapeDtypeStruct((tokens, dim), BF16)] * 2,
        compiler_params=params(),
        name="key_side",
    )(valid, kv, qg, rows)


def swap_mate(value):
    count = lax.axis_size("tm")
    return lax.ppermute(value, "tm", [(source, source ^ 1) for source in range(count)])


def swap_cross(value):
    count = lax.axis_size("tm")
    return lax.ppermute(value, "tm", [(s, cross_of(s)) for s in range(count) if has_cross(s % ROW_TILES)])


def cross_of(index):
    return index + 1 if index % CHIP_ROWS == CHIP_ROWS - 1 else index - 1


def has_cross(row):
    return 0 <= cross_of(row) < ROW_TILES


def shift_frame(value, steps, cross_only=False):
    count = lax.axis_size("tm")
    pairs = [(s, s + steps * ROW_TILES) for s in range(count) if 0 <= s + steps * ROW_TILES < count]
    if cross_only:
        pairs = [pair for pair in pairs if has_cross(pair[0] % ROW_TILES)]
    return lax.ppermute(value, "tm", pairs)


def neighbours(value):
    before = shift_frame(value, 1)
    after = shift_frame(value, -1)
    cross = swap_cross(value)
    mate = swap_mate(value)
    cross_before = shift_frame(cross, 1, True)
    cross_after = shift_frame(cross, -1, True)
    mate_before = swap_mate(before)
    mate_after = swap_mate(after)
    return [value, mate, cross, before, after, mate_before, mate_after, cross_before, cross_after]


def row_neighbours(rows):
    trio = jnp.stack([rows, swap_mate(rows), swap_cross(rows)])
    before = shift_frame(trio, 1)
    after = shift_frame(trio, -1)
    return jnp.stack([trio[0], trio[1], trio[2], before[0], after[0], before[1], after[1], before[2], after[2]])


def per_device(queries, key_codes, value_codes, key_scales, value_scales, scale_slot, grad_out):
    index = lax.axis_index("tm")
    frames = lax.axis_size("tm") // ROW_TILES
    frame = index // ROW_TILES
    row = index % ROW_TILES
    before = (frame > 0).astype(jnp.int32)
    after = (frame < frames - 1).astype(jnp.int32)
    cross = functools.reduce(lax.bitwise_or, [row == r for r in range(ROW_TILES) if has_cross(r)]).astype(jnp.int32)
    one = jnp.ones((), jnp.int32)
    valid = jnp.stack([one, one, cross, before, after, before, after, cross * before, cross * after])

    kv, qg = prepare(queries, key_codes, value_codes, key_scales, value_scales, scale_slot, grad_out)
    kv_list = neighbours(kv)
    qg_later, kv_list[3], kv_list[4] = lax.optimization_barrier((qg, kv_list[3], kv_list[4]))
    qg_list = neighbours(qg_later)

    tokens = queries.shape[0]
    zeros = jnp.zeros((8, tokens), F32)
    start = jnp.stack([zeros + BIG_NEGATIVE, zeros, zeros])
    (running,) = stats(valid[:5], qg, jnp.stack(kv_list[:5]), start, False)
    _, rows = stats(valid[5:], qg, jnp.stack(kv_list[5:]), running, True)
    rows_all = row_neighbours(rows)
    query_grad = query_side(valid, qg, jnp.stack(kv_list), rows)
    key_grad, value_grad = key_side(valid, kv, jnp.stack(qg_list), rows_all)
    return query_grad, key_grad, value_grad


def solution(mesh):
    whole_axis = ("grp", "tm")
    flat = P(whole_axis)
    split = P(whole_axis, None)
    return jax.shard_map(
        per_device,
        mesh=mesh,
        in_specs=(split, split, split, flat, flat, split, split),
        out_specs=(split, split, split),
        check_vma=False,
    )
```

```python
import functools
import math

import jax
import jax.numpy as jnp
from jax import lax
from jax.experimental import pallas as pl
from jax.experimental.pallas import tpu as pltpu
from jax.sharding import PartitionSpec as P

HEAD_DIM = 128
TILE_TOKENS = 256
ROW_TILES = 4
CHIP_ROWS = 2

SCALE = HEAD_DIM ** (-0.5)
SCALE2 = SCALE * math.log2(math.e)
BIG_NEGATIVE = -1e30
STATS_KEYS = 128
VMEM_LIMIT = 48 * 2**20

F32 = jnp.float32
BF16 = jnp.bfloat16
NT = (((1,), (1,)), ((), ()))
TN = (((0,), (0,)), ((), ()))
NN = (((1,), (0,)), ((), ()))


def dot(left, right, dims):
    return lax.dot_general(left, right, dims, preferred_element_type=F32)


def near(tile, tokens):
    return max(0, tile - 1) * TILE_TOKENS, min(tokens, (tile + 2) * TILE_TOKENS)


def params():
    return pltpu.CompilerParams(vmem_limit_bytes=VMEM_LIMIT)


def cost(products, slabs, tokens, dim):
    pairs = slabs * tokens * tokens
    return pl.CostEstimate(flops=8 * products * pairs * dim, bytes_accessed=slabs * 4 * tokens * dim, transcendentals=pairs)


def prepare_kernel(key_scales, value_scales, slots, queries, key_codes, value_codes, grad_out, kv, qg,
                   scale_mem, slot_mem, codes, packed, sems):
    blocks = slots.shape[1]
    size = queries.shape[0] // blocks
    loads = [
        pltpu.make_async_copy(key_scales, scale_mem.at[0], sems.at[0]),
        pltpu.make_async_copy(value_scales, scale_mem.at[1], sems.at[1]),
        pltpu.make_async_copy(slots.at[0], slot_mem, sems.at[2]),
        pltpu.make_async_copy(key_codes, codes.at[0], sems.at[3]),
        pltpu.make_async_copy(value_codes, codes.at[1], sems.at[4]),
        pltpu.make_async_copy(queries, packed.at[2], sems.at[5]),
        pltpu.make_async_copy(grad_out, packed.at[3], sems.at[6]),
    ]
    for load in loads:
        load.start()
    for load in loads[:5]:
        load.wait()
    for block in range(blocks):
        rows = slice(block * size, (block + 1) * size)
        slot = slot_mem[block]
        for part in range(2):
            packed[part, rows] = (codes[part, rows].astype(F32) * scale_mem[part, slot]).astype(BF16)
    stores = [pltpu.make_async_copy(packed.at[0:2], kv, sems.at[7])]
    stores[0].start()
    for load in loads[5:]:
        load.wait()
    stores.append(pltpu.make_async_copy(packed.at[2:4], qg, sems.at[8]))
    stores[1].start()
    for store in stores:
        store.wait()


def prepare(queries, key_codes, value_codes, key_scales, value_scales, slots, grad_out):
    blocks = slots.shape[1]
    anywhere = pl.BlockSpec(memory_space=pl.ANY)
    return pl.pallas_call(
        prepare_kernel,
        in_specs=[anywhere] * 7,
        out_specs=[anywhere] * 2,
        out_shape=[jax.ShapeDtypeStruct((n,) + queries.shape, BF16) for n in (2, 2)],
        scratch_shapes=[
            pltpu.SMEM((2, blocks), F32),
            pltpu.SMEM((blocks,), jnp.int32),
            pltpu.VMEM((2,) + queries.shape, BF16),
            pltpu.VMEM((4,) + queries.shape, BF16),
            pltpu.SemaphoreType.DMA((9,)),
        ],
        compiler_params=pltpu.CompilerParams(vmem_limit_bytes=60 * 2**20),
        name="prepare",
    )(key_scales, value_scales, slots, queries, key_codes, value_codes, grad_out)


def vmem_call(kernel, name, products, slabs, outs, scratch, *operands):
    tokens, dim = operands[1].shape[1:]
    vmem = pl.BlockSpec(memory_space=pltpu.VMEM)
    return pl.pallas_call(
        kernel,
        in_specs=[pl.BlockSpec(memory_space=pltpu.SMEM)] + [vmem] * (len(operands) - 1),
        out_specs=[vmem] * len(outs),
        out_shape=outs,
        scratch_shapes=scratch,
        cost_estimate=cost(products, slabs, tokens, dim),
        compiler_params=params(),
        name=name,
    )(*operands)


def arrays_of(window):
    arrays = []
    for array, _ in window:
        if not any(array is other for other in arrays):
            arrays.append(array)
    places = [([array is other for other in arrays].index(True), offset) for array, offset in window]
    return arrays, places


def for_each_slab(valid, first, places, refs, body):
    for number, (place, offset) in enumerate(places):

        @pl.when(valid[first + number] > 0)
        def _(ref=refs[place], offset=offset, number=number):
            body(number, lambda part, rows: ref[offset + part, rows])


def stats_kernel(first, places, finish, valid, qg, start, *refs):
    tokens = qg.shape[1]
    running = refs[-1]
    running[...] = start[...]

    def body(number, part):
        for tile in range(tokens // TILE_TOKENS):
            cols = slice(tile * TILE_TOKENS, (tile + 1) * TILE_TOKENS)
            low, high = near(tile, tokens)
            shape = (STATS_KEYS // 8, 8, TILE_TOKENS)
            top, total, weighted = running[0, :, cols], running[1, :, cols], running[2, :, cols]
            for key in range(low, high, STATS_KEYS):
                keys = slice(key, key + STATS_KEYS)
                scores = (dot(part(0, keys), qg[0, cols], NT) * SCALE2).reshape(shape)
                grad_prob = dot(part(1, keys), qg[1, cols], NT).reshape(shape)
                new_top = jnp.maximum(top, jnp.max(scores, axis=0))
                unscaled = jnp.exp2(scores - new_top[None])
                rescale = jnp.exp2(top - new_top)
                top = new_top
                total = total * rescale + jnp.sum(unscaled, axis=0)
                weighted = weighted * rescale + jnp.sum(unscaled * grad_prob, axis=0)
            running[0, :, cols], running[1, :, cols], running[2, :, cols] = top, total, weighted

    for_each_slab(valid, first, places, refs, body)
    if finish:
        final = refs[-2]
        top = running[0]
        row_top = jnp.max(top, axis=0, keepdims=True)
        rescale = jnp.exp2(top - row_top)
        total = jnp.sum(running[1] * rescale, axis=0, keepdims=True)
        weighted = jnp.sum(running[2] * rescale, axis=0, keepdims=True)
        final[0:1] = row_top + jnp.log2(total)
        final[1:2] = weighted / total


def stats(valid, first, qg, window, start, finish):
    tokens = qg.shape[1]
    arrays, places = arrays_of(window)
    running = (3, 8, tokens)
    outs = jax.ShapeDtypeStruct((2, tokens) if finish else running, F32)
    return vmem_call(
        functools.partial(stats_kernel, first, places, finish), "row_stats", 2, len(window),
        [outs], [pltpu.VMEM(running, F32)] if finish else [], valid, qg, start, *arrays,
    )[0]


def query_kernel(places, valid, qg, rows, *refs):
    out, total = refs[-2:]
    tokens = qg.shape[1]
    total[...] = jnp.zeros_like(total)

    def body(number, part):
        for tile in range(tokens // TILE_TOKENS):
            cols = slice(tile * TILE_TOKENS, (tile + 1) * TILE_TOKENS)
            low, high = near(tile, tokens)
            keys = part(0, slice(low, high))
            scores = dot(keys, qg[0, cols], NT)
            attn_prob = jnp.exp2(scores * SCALE2 - rows[0:1, cols])
            grad_prob = dot(part(1, slice(low, high)), qg[1, cols], NT)
            dscore = (attn_prob * (grad_prob - rows[1:2, cols])).astype(BF16)
            total[:, cols] += dot(keys, dscore, TN)

    for_each_slab(valid, 0, places, refs, body)
    out[...] = (total[...] * SCALE).T.astype(BF16)


def query_side(valid, qg, window, rows):
    tokens, dim = qg.shape[1:]
    arrays, places = arrays_of(window)
    return vmem_call(
        functools.partial(query_kernel, places), "query_side", 3, len(window),
        [jax.ShapeDtypeStruct((tokens, dim), BF16)], [pltpu.VMEM((dim, tokens), F32)], valid, qg, rows, *arrays,
    )[0]


def key_kernel(places, valid, kv, rows, *refs):
    key_out, value_out, totals = refs[-3:]
    tokens = kv.shape[1]
    totals[...] = jnp.zeros_like(totals)

    def body(number, part):
        for tile in range(tokens // TILE_TOKENS):
            cols = slice(tile * TILE_TOKENS, (tile + 1) * TILE_TOKENS)
            low, high = near(tile, tokens)
            queries = part(0, slice(low, high))
            grads = part(1, slice(low, high))
            scores = dot(kv[0, cols], queries, NT)
            attn_prob = jnp.exp2(scores * SCALE2 - rows[number, 0:1, low:high])
            grad_prob = dot(kv[1, cols], grads, NT)
            dscore = (attn_prob * (grad_prob - rows[number, 1:2, low:high])).astype(BF16)
            key_part = (dot(dscore, queries, NN) * SCALE).astype(BF16)
            value_part = dot(attn_prob.astype(BF16), grads, NN).astype(BF16)
            totals[0, cols] += key_part.astype(F32)
            totals[1, cols] += value_part.astype(F32)

    for_each_slab(valid, 0, places, refs, body)
    key_out[...] = totals[0].astype(BF16)
    value_out[...] = totals[1].astype(BF16)


def key_side(valid, kv, window, rows):
    tokens, dim = kv.shape[1:]
    arrays, places = arrays_of(window)
    return vmem_call(
        functools.partial(key_kernel, places), "key_side", 4, len(window),
        [jax.ShapeDtypeStruct((tokens, dim), BF16)] * 2, [pltpu.VMEM((2, tokens, dim), F32)], valid, kv, rows, *arrays,
    )


def swap_mate(value):
    count = lax.axis_size("tm")
    return lax.ppermute(value, "tm", [(source, source ^ 1) for source in range(count)])


def swap_cross(value):
    count = lax.axis_size("tm")
    return lax.ppermute(value, "tm", [(s, cross_of(s)) for s in range(count) if has_cross(s % ROW_TILES)])


def cross_of(index):
    return index + 1 if index % CHIP_ROWS == CHIP_ROWS - 1 else index - 1


def has_cross(row):
    return 0 <= cross_of(row) < ROW_TILES


def shift_frame(value, steps, cross_only=False):
    count = lax.axis_size("tm")
    pairs = [(s, s + steps * ROW_TILES) for s in range(count) if 0 <= s + steps * ROW_TILES < count]
    if cross_only:
        pairs = [pair for pair in pairs if has_cross(pair[0] % ROW_TILES)]
    return lax.ppermute(value, "tm", pairs)


def row_neighbours(rows):
    trio = jnp.stack([rows, swap_mate(rows), swap_cross(rows)])
    before = shift_frame(trio, 1)
    after = shift_frame(trio, -1)
    return jnp.stack([trio[0], trio[1], trio[2], before[0], after[0], before[1], after[1], before[2], after[2]])


def per_device(queries, key_codes, value_codes, key_scales, value_scales, scale_slot, grad_out):
    index = lax.axis_index("tm")
    frames = lax.axis_size("tm") // ROW_TILES
    frame = index // ROW_TILES
    row = index % ROW_TILES
    before = (frame > 0).astype(jnp.int32)
    after = (frame < frames - 1).astype(jnp.int32)
    cross = functools.reduce(lax.bitwise_or, [row == r for r in range(ROW_TILES) if has_cross(r)]).astype(jnp.int32)
    one = jnp.ones((), jnp.int32)
    valid = jnp.stack([one, one, cross, before, after, before, after, cross * before, cross * after])

    kv, qg = prepare(queries, key_codes, value_codes, key_scales, value_scales, scale_slot, grad_out)
    kv_before = shift_frame(kv, 1)
    kv_after = shift_frame(kv, -1)
    kv_cross = swap_cross(kv)
    kv_mate = swap_mate(kv)
    qg_cross = swap_cross(qg)
    kv_cross_before = shift_frame(kv_cross, 1, True)
    kv_cross_after = shift_frame(kv_cross, -1, True)
    kv_mate_before = swap_mate(kv_before)
    kv_mate_after = swap_mate(kv_after)

    qg_pair, _, _ = lax.optimization_barrier((jnp.concatenate([qg, qg_cross]), kv_before, kv_after))
    qg_before = shift_frame(qg_pair, 1)
    qg_after = shift_frame(qg_pair, -1)
    qg_mate = swap_mate(qg)
    qg_mate_before = swap_mate(qg_before)
    qg_mate_after = swap_mate(qg_after)
    qg_window = [(qg, 0), (qg_mate, 0), (qg_cross, 0), (qg_before, 0), (qg_after, 0),
                 (qg_mate_before, 0), (qg_mate_after, 0), (qg_before, 2), (qg_after, 2)]

    tokens = queries.shape[0]
    zeros = jnp.zeros((8, tokens), F32)
    running = jnp.stack([zeros + BIG_NEGATIVE, zeros, zeros])
    groups = [
        [(kv, 0), (kv_mate, 0)],
        [(kv_cross, 0), (kv_before, 0), (kv_after, 0)],
        [(kv_mate_before, 0), (kv_mate_after, 0), (kv_cross_before, 0), (kv_cross_after, 0)],
    ]
    running = stats(valid, 0, qg, groups[0], running, False)
    running = stats(valid, 2, qg, groups[1], running, False)
    rows = stats(valid, 5, qg, groups[2], running, True)
    rows_all = row_neighbours(rows)
    query_grad = query_side(valid, qg, groups[0] + groups[1] + groups[2], rows)
    key_grad, value_grad = key_side(valid, kv, qg_window, rows_all)
    return query_grad, key_grad, value_grad


def solution(mesh):
    whole_axis = ("grp", "tm")
    flat = P(whole_axis)
    split = P(whole_axis, None)
    return jax.shard_map(
        per_device,
        mesh=mesh,
        in_specs=(split, split, split, flat, flat, split, split),
        out_specs=(split, split, split),
        check_vma=False,
    )
```

```python
import functools
import math

import jax
import jax.numpy as jnp
from jax import lax
from jax.experimental import pallas as pl
from jax.experimental.pallas import tpu as pltpu
from jax.sharding import PartitionSpec as P

HEAD_DIM = 128
TILE_TOKENS = 256
ROW_TILES = 4
CHIP_ROWS = 2

SCALE = HEAD_DIM ** (-0.5)
SCALE2 = SCALE * math.log2(math.e)
BIG_NEGATIVE = -1e30
STATS_KEYS = 128
VMEM_LIMIT = 48 * 2**20

F32 = jnp.float32
BF16 = jnp.bfloat16
NT = (((1,), (1,)), ((), ()))
TN = (((0,), (0,)), ((), ()))
NN = (((1,), (0,)), ((), ()))


def dot(left, right, dims):
    return lax.dot_general(left, right, dims, preferred_element_type=F32)


def near(tile, tokens):
    return max(0, tile - 1) * TILE_TOKENS, min(tokens, (tile + 2) * TILE_TOKENS)


def params():
    return pltpu.CompilerParams(vmem_limit_bytes=VMEM_LIMIT)


def cost(products, slabs, tokens, dim):
    pairs = slabs * tokens * tokens
    return pl.CostEstimate(flops=products * pairs * dim, bytes_accessed=slabs * tokens * dim, transcendentals=0)


def prepare_kernel(key_scales, value_scales, slots, queries, key_codes, value_codes, grad_out, kv, qg,
                   scale_mem, slot_mem, codes, sems):
    blocks = slots.shape[1]
    size = queries.shape[0] // blocks
    loads = [
        pltpu.make_async_copy(key_scales, scale_mem.at[0], sems.at[0]),
        pltpu.make_async_copy(value_scales, scale_mem.at[1], sems.at[1]),
        pltpu.make_async_copy(slots.at[0], slot_mem, sems.at[2]),
        pltpu.make_async_copy(key_codes, codes.at[0], sems.at[3]),
        pltpu.make_async_copy(value_codes, codes.at[1], sems.at[4]),
        pltpu.make_async_copy(queries, qg.at[0], sems.at[5]),
        pltpu.make_async_copy(grad_out, qg.at[1], sems.at[6]),
    ]
    for load in loads:
        load.start()
    for load in loads[:5]:
        load.wait()
    for block in range(blocks):
        rows = slice(block * size, (block + 1) * size)
        slot = slot_mem[block]
        for part in range(2):
            kv[part, rows] = (codes[part, rows].astype(F32) * scale_mem[part, slot]).astype(BF16)
    for load in loads[5:]:
        load.wait()


def prepare(queries, key_codes, value_codes, key_scales, value_scales, slots, grad_out):
    blocks = slots.shape[1]
    anywhere = pl.BlockSpec(memory_space=pl.ANY)
    return pl.pallas_call(
        prepare_kernel,
        in_specs=[anywhere] * 7,
        out_specs=[pl.BlockSpec(memory_space=pltpu.VMEM)] * 2,
        out_shape=[jax.ShapeDtypeStruct((n,) + queries.shape, BF16) for n in (2, 2)],
        scratch_shapes=[
            pltpu.SMEM((2, blocks), F32),
            pltpu.SMEM((blocks,), jnp.int32),
            pltpu.VMEM((2,) + queries.shape, BF16),
            pltpu.SemaphoreType.DMA((7,)),
        ],
        compiler_params=pltpu.CompilerParams(vmem_limit_bytes=60 * 2**20),
        name="prepare",
    )(key_scales, value_scales, slots, queries, key_codes, value_codes, grad_out)


def vmem_call(kernel, name, products, slabs, outs, scratch, *operands):
    tokens, dim = operands[1].shape[1:]
    vmem = pl.BlockSpec(memory_space=pltpu.VMEM)
    return pl.pallas_call(
        kernel,
        in_specs=[pl.BlockSpec(memory_space=pltpu.SMEM)] + [vmem] * (len(operands) - 1),
        out_specs=[vmem] * len(outs),
        out_shape=outs,
        scratch_shapes=scratch,
        cost_estimate=cost(products, slabs, tokens, dim),
        compiler_params=params(),
        name=name,
    )(*operands)


def arrays_of(window):
    arrays = []
    for array, _ in window:
        if not any(array is other for other in arrays):
            arrays.append(array)
    places = [([array is other for other in arrays].index(True), offset) for array, offset in window]
    return arrays, places


def for_each_slab(valid, first, places, refs, body):
    for number, (place, offset) in enumerate(places):

        @pl.when(valid[first + number] > 0)
        def _(ref=refs[place], offset=offset, number=number):
            body(number, lambda part, rows: ref[offset + part, rows])


def stats_kernel(first, places, finish, valid, qg, start, *refs):
    tokens = qg.shape[1]
    running = refs[-1]
    running[...] = start[...]

    def body(number, part):
        for tile in range(tokens // TILE_TOKENS):
            cols = slice(tile * TILE_TOKENS, (tile + 1) * TILE_TOKENS)
            low, high = near(tile, tokens)
            shape = (STATS_KEYS // 8, 8, TILE_TOKENS)
            top, total, weighted = running[0, :, cols], running[1, :, cols], running[2, :, cols]
            for key in range(low, high, STATS_KEYS):
                keys = slice(key, key + STATS_KEYS)
                scores = (dot(part(0, keys), qg[0, cols], NT) * SCALE2).reshape(shape)
                grad_prob = dot(part(1, keys), qg[1, cols], NT).reshape(shape)
                new_top = jnp.maximum(top, jnp.max(scores, axis=0))
                unscaled = jnp.exp2(scores - new_top[None])
                rescale = jnp.exp2(top - new_top)
                top = new_top
                total = total * rescale + jnp.sum(unscaled, axis=0)
                weighted = weighted * rescale + jnp.sum(unscaled * grad_prob, axis=0)
            running[0, :, cols], running[1, :, cols], running[2, :, cols] = top, total, weighted

    for_each_slab(valid, first, places, refs, body)
    if finish:
        final = refs[-2]
        top = running[0]
        row_top = jnp.max(top, axis=0, keepdims=True)
        rescale = jnp.exp2(top - row_top)
        total = jnp.sum(running[1] * rescale, axis=0, keepdims=True)
        weighted = jnp.sum(running[2] * rescale, axis=0, keepdims=True)
        final[0:1] = row_top + jnp.log2(total)
        final[1:2] = weighted / total


def stats(valid, first, qg, window, start, finish):
    tokens = qg.shape[1]
    arrays, places = arrays_of(window)
    running = (3, 8, tokens)
    outs = jax.ShapeDtypeStruct((2, tokens) if finish else running, F32)
    return vmem_call(
        functools.partial(stats_kernel, first, places, finish), "row_stats", 2, len(window),
        [outs], [pltpu.VMEM(running, F32)] if finish else [], valid, qg, start, *arrays,
    )[0]


def query_kernel(first, places, finish, valid, qg, rows, start, *refs):
    total = refs[-1]
    tokens = qg.shape[1]
    total[...] = start[...]

    def body(number, part):
        for tile in range(tokens // TILE_TOKENS):
            cols = slice(tile * TILE_TOKENS, (tile + 1) * TILE_TOKENS)
            low, high = near(tile, tokens)
            keys = part(0, slice(low, high))
            scores = dot(keys, qg[0, cols], NT)
            attn_prob = jnp.exp2(scores * SCALE2 - rows[0:1, cols])
            grad_prob = dot(part(1, slice(low, high)), qg[1, cols], NT)
            dscore = (attn_prob * (grad_prob - rows[1:2, cols])).astype(BF16)
            total[:, cols] += dot(keys, dscore, TN)

    for_each_slab(valid, first, places, refs, body)
    if finish:
        refs[-2][...] = (total[...] * SCALE).T.astype(BF16)


def query_side(valid, first, qg, window, rows, start, finish):
    tokens, dim = qg.shape[1:]
    arrays, places = arrays_of(window)
    outs = jax.ShapeDtypeStruct((tokens, dim), BF16) if finish else jax.ShapeDtypeStruct((dim, tokens), F32)
    return vmem_call(
        functools.partial(query_kernel, first, places, finish), "query_side", 3, len(window),
        [outs], [pltpu.VMEM((dim, tokens), F32)] if finish else [], valid, qg, rows, start, *arrays,
    )[0]


def key_kernel(first, places, finish, valid, kv, rows, start, *refs):
    totals = refs[-1]
    tokens = kv.shape[1]
    totals[...] = start[...]

    def body(number, part):
        for tile in range(tokens // TILE_TOKENS):
            cols = slice(tile * TILE_TOKENS, (tile + 1) * TILE_TOKENS)
            low, high = near(tile, tokens)
            queries = part(0, slice(low, high))
            grads = part(1, slice(low, high))
            scores = dot(kv[0, cols], queries, NT)
            attn_prob = jnp.exp2(scores * SCALE2 - rows[first + number, 0:1, low:high])
            grad_prob = dot(kv[1, cols], grads, NT)
            dscore = (attn_prob * (grad_prob - rows[first + number, 1:2, low:high])).astype(BF16)
            key_part = (dot(dscore, queries, NN) * SCALE).astype(BF16)
            value_part = dot(attn_prob.astype(BF16), grads, NN).astype(BF16)
            totals[0, cols] += key_part.astype(F32)
            totals[1, cols] += value_part.astype(F32)

    for_each_slab(valid, first, places, refs, body)
    if finish:
        refs[-3][...] = totals[0].astype(BF16)
        refs[-2][...] = totals[1].astype(BF16)


def key_side(valid, first, kv, window, rows, start, finish):
    tokens, dim = kv.shape[1:]
    arrays, places = arrays_of(window)
    totals = (2, tokens, dim)
    outs = [jax.ShapeDtypeStruct((tokens, dim), BF16)] * 2 if finish else [jax.ShapeDtypeStruct(totals, F32)]
    return vmem_call(
        functools.partial(key_kernel, first, places, finish), "key_side", 4, len(window),
        outs, [pltpu.VMEM(totals, F32)] if finish else [], valid, kv, rows, start, *arrays,
    )


def swap_mate(value):
    count = lax.axis_size("tm")
    return lax.ppermute(value, "tm", [(source, source ^ 1) for source in range(count)])


def swap_cross(value):
    count = lax.axis_size("tm")
    return lax.ppermute(value, "tm", [(s, cross_of(s)) for s in range(count) if has_cross(s % ROW_TILES)])


def cross_of(index):
    return index + 1 if index % CHIP_ROWS == CHIP_ROWS - 1 else index - 1


def has_cross(row):
    return 0 <= cross_of(row) < ROW_TILES


def frame_step(frame, phase):
    return 1 - 2 * ((frame + phase) % 2)


def swap_frames(value, phase, cross_only=False):
    count = lax.axis_size("tm")
    pairs = [(s, s + frame_step(s // ROW_TILES, phase) * ROW_TILES) for s in range(count)]
    pairs = [pair for pair in pairs if 0 <= pair[1] < count]
    if cross_only:
        pairs = [pair for pair in pairs if has_cross(pair[0] % ROW_TILES)]
    return lax.ppermute(value, "tm", pairs)


def per_device(queries, key_codes, value_codes, key_scales, value_scales, scale_slot, grad_out):
    index = lax.axis_index("tm")
    frames = lax.axis_size("tm") // ROW_TILES
    frame = index // ROW_TILES
    row = index % ROW_TILES
    cross = functools.reduce(lax.bitwise_or, [row == r for r in range(ROW_TILES) if has_cross(r)]).astype(jnp.int32)
    others = [frame + frame_step(frame, phase) for phase in range(2)]
    frame_a, frame_b = [((other >= 0) & (other < frames)).astype(jnp.int32) for other in others]
    one = jnp.ones((), jnp.int32)
    valid = jnp.stack([one, one, cross, frame_a, frame_b, cross * frame_a, cross * frame_b, frame_a, frame_b])

    kv, qg = prepare(queries, key_codes, value_codes, key_scales, value_scales, scale_slot, grad_out)
    kv_a = swap_frames(kv, 0)
    kv_b = swap_frames(kv, 1)
    kv_cross = swap_cross(kv)
    kv_mate = swap_mate(kv)
    qg_cross = swap_cross(qg)
    kv_cross_a = swap_frames(kv_cross, 0, True)
    kv_cross_b = swap_frames(kv_cross, 1, True)
    kv_mate_a = swap_mate(kv_a)
    kv_mate_b = swap_mate(kv_b)

    qg_pair, _, _ = lax.optimization_barrier((jnp.concatenate([qg, qg_cross]), kv_a, kv_b))
    qg_a = swap_frames(qg_pair, 0)
    qg_b = swap_frames(qg_pair, 1)
    qg_mate = swap_mate(qg)
    qg_mate_a = swap_mate(qg_a)
    qg_mate_b = swap_mate(qg_b)

    tokens, dim = queries.shape
    kv_near = [(kv, 0), (kv_mate, 0)]
    kv_next = [(kv_cross, 0), (kv_a, 0), (kv_b, 0)]
    kv_last = [(kv_cross_a, 0), (kv_cross_b, 0), (kv_mate_a, 0), (kv_mate_b, 0)]
    zeros = jnp.zeros((8, tokens), F32)
    running = jnp.stack([zeros + BIG_NEGATIVE, zeros, zeros])
    running = stats(valid, 0, qg, kv_near, running, False)
    running = stats(valid, 2, qg, kv_next, running, False)
    rows = stats(valid, 5, qg, kv_last, running, True)

    trio = jnp.stack([rows, swap_mate(rows), swap_cross(rows)])
    query_total = query_side(valid, 0, qg, kv_near + kv_next, rows, jnp.zeros((dim, tokens), F32), False)
    trio, query_total = lax.optimization_barrier((trio, query_total))
    trio_a = swap_frames(trio, 0)
    trio_b = swap_frames(trio, 1)
    query_grad = query_side(valid, 5, qg, kv_last, rows, query_total, True)

    rows_all = jnp.stack([trio[0], trio[1], trio[2], trio_a[0], trio_b[0], trio_a[2], trio_b[2], trio_a[1], trio_b[1]])
    qg_first = [(qg, 0), (qg_mate, 0), (qg_cross, 0), (qg_a, 0), (qg_b, 0), (qg_a, 2), (qg_b, 2)]
    qg_last = [(qg_mate_a, 0), (qg_mate_b, 0)]
    (totals,) = key_side(valid, 0, kv, qg_first, rows_all, jnp.zeros((2, tokens, dim), F32), False)
    key_grad, value_grad = key_side(valid, 7, kv, qg_last, rows_all, totals, True)
    return query_grad, key_grad, value_grad


def solution(mesh):
    whole_axis = ("grp", "tm")
    flat = P(whole_axis)
    split = P(whole_axis, None)
    return jax.shard_map(
        per_device,
        mesh=mesh,
        in_specs=(split, split, split, flat, flat, split, split),
        out_specs=(split, split, split),
        check_vma=False,
    )
```

```python
import functools
import math

import jax
import jax.numpy as jnp
from jax import lax
from jax.experimental import pallas as pl
from jax.experimental.pallas import tpu as pltpu
from jax.sharding import PartitionSpec as P

HEAD_DIM = 128
TILE_TOKENS = 256
ROW_TILES = 4
CHIP_ROWS = 2

SCALE = HEAD_DIM ** (-0.5)
SCALE2 = SCALE * math.log2(math.e)
BIG_NEGATIVE = -1e30
STATS_KEYS = 128
VMEM_LIMIT = 8 * 2**20

F32 = jnp.float32
BF16 = jnp.bfloat16
NT = (((1,), (1,)), ((), ()))
TN = (((0,), (0,)), ((), ()))
NN = (((1,), (0,)), ((), ()))


def dot(left, right, dims):
    return lax.dot_general(left, right, dims, preferred_element_type=F32)


def near(tile, tokens):
    return max(0, tile - 1) * TILE_TOKENS, min(tokens, (tile + 2) * TILE_TOKENS)


def params():
    return pltpu.CompilerParams(vmem_limit_bytes=VMEM_LIMIT)


def cost(products, slabs, tokens, dim):
    pairs = slabs * tokens * tokens
    return pl.CostEstimate(flops=products * pairs * dim, bytes_accessed=slabs * tokens * dim, transcendentals=0)


def prepare(queries, key_codes, value_codes, key_scales, value_scales, scale_slot, grad_out):
    tokens, dim = queries.shape
    blocks = scale_slot.shape[1]
    picker = scale_slot[0][:, None] == jnp.arange(blocks, dtype=jnp.int32)[None, :]

    def scaled(codes, scales):
        picked = jnp.sum(jnp.where(picker, scales[None, :], 0.0), axis=1)
        blocked = codes.astype(F32).reshape(blocks, tokens // blocks, dim)
        return (blocked * picked[:, None, None]).astype(BF16).reshape(tokens, dim)

    kv = jnp.stack([scaled(key_codes, key_scales), scaled(value_codes, value_scales)])
    return kv, jnp.stack([queries, grad_out])


def vmem_call(kernel, name, products, slabs, outs, scratch, *operands):
    tokens, dim = operands[-1].shape[1:]
    vmem = pl.BlockSpec(memory_space=pltpu.VMEM)
    return pl.pallas_call(
        kernel,
        in_specs=[pl.BlockSpec(memory_space=pltpu.SMEM)] + [vmem] * (len(operands) - 1),
        out_specs=[vmem] * len(outs),
        out_shape=outs,
        scratch_shapes=scratch,
        cost_estimate=cost(products, slabs, tokens, dim),
        compiler_params=params(),
        name=name,
    )(*operands)


def arrays_of(window):
    arrays = []
    for array, _ in window:
        if not any(array is other for other in arrays):
            arrays.append(array)
    places = [([array is other for other in arrays].index(True), offset) for array, offset in window]
    return arrays, places


def for_each_slab(valid, first, places, refs, body):
    for number, (place, offset) in enumerate(places):

        @pl.when(valid[first + number] > 0)
        def _(ref=refs[place], offset=offset, number=number):
            body(number, lambda part, rows: ref[offset + part, rows])


def tile_pairs(tokens):
    tiles = tokens // TILE_TOKENS
    return [(tile, key) for tile in range(tiles) for key in range(max(0, tile - 1), min(tiles, tile + 2))]


def stats_kernel(first, places, finish, valid, qg, *refs):
    tokens = qg.shape[1]
    running, kept = refs[-1], refs[-2]
    if first == 0:
        running[0] = jnp.full(running.shape[1:], BIG_NEGATIVE, F32)
        running[1:] = jnp.zeros((2,) + running.shape[1:], F32)
    else:
        running[...] = refs[0][...]
        refs = refs[1:]
    shape = (STATS_KEYS // 8, 8, TILE_TOKENS)

    def body(number, part):
        for tile in range(tokens // TILE_TOKENS):
            cols = slice(tile * TILE_TOKENS, (tile + 1) * TILE_TOKENS)
            top, total, weighted = running[0, :, cols], running[1, :, cols], running[2, :, cols]
            for place, pair in enumerate(tile_pairs(tokens)):
                if pair[0] != tile:
                    continue
                for key in range(0, TILE_TOKENS, STATS_KEYS):
                    inner = slice(key, key + STATS_KEYS)
                    keys = slice(pair[1] * TILE_TOKENS + key, pair[1] * TILE_TOKENS + key + STATS_KEYS)
                    scores = dot(part(0, keys), qg[0, cols], NT) * SCALE2
                    grad_prob = dot(part(1, keys), qg[1, cols], NT)
                    kept[number, place, 0, inner] = scores
                    kept[number, place, 1, inner] = grad_prob
                    scores = scores.reshape(shape)
                    new_top = jnp.maximum(top, jnp.max(scores, axis=0))
                    unscaled = jnp.exp2(scores - new_top[None])
                    rescale = jnp.exp2(top - new_top)
                    top = new_top
                    total = total * rescale + jnp.sum(unscaled, axis=0)
                    weighted = weighted * rescale + jnp.sum(unscaled * grad_prob.reshape(shape), axis=0)
            running[0, :, cols], running[1, :, cols], running[2, :, cols] = top, total, weighted

    for_each_slab(valid, first, places, refs, body)
    if finish:
        final = refs[-3]
        top = running[0]
        row_top = jnp.max(top, axis=0, keepdims=True)
        rescale = jnp.exp2(top - row_top)
        total = jnp.sum(running[1] * rescale, axis=0, keepdims=True)
        weighted = jnp.sum(running[2] * rescale, axis=0, keepdims=True)
        final[0:1] = row_top + jnp.log2(total)
        final[1:2] = weighted / total


def stats(valid, first, qg, window, start, finish):
    tokens = qg.shape[1]
    arrays, places = arrays_of(window)
    running = (3, 8, tokens)
    kept = jax.ShapeDtypeStruct((len(window), len(tile_pairs(tokens)), 2, TILE_TOKENS, TILE_TOKENS), F32)
    result = jax.ShapeDtypeStruct((2, tokens) if finish else running, F32)
    outs = vmem_call(
        functools.partial(stats_kernel, first, places, finish), "row_stats", 2, len(window),
        [result, kept] if finish else [kept, result], [pltpu.VMEM(running, F32)] if finish else [],
        valid, qg, *([] if first == 0 else [start]), *arrays,
    )
    return outs if finish else outs[::-1]


def query_kernel(places, groups, valid, rows, *refs):
    out, total = refs[-2:]
    tokens = rows.shape[1]
    total[...] = jnp.zeros_like(total)
    kept = [(ref, number) for ref in refs[:groups] for number in range(ref.shape[0])]

    def body(number, part):
        scores, index = kept[number]
        for tile in range(tokens // TILE_TOKENS):
            cols = slice(tile * TILE_TOKENS, (tile + 1) * TILE_TOKENS)
            low, high = near(tile, tokens)
            dscores = []
            for place, pair in enumerate(tile_pairs(tokens)):
                if pair[0] == tile:
                    attn_prob = jnp.exp2(scores[index, place, 0] - rows[0:1, cols])
                    dscores.append((attn_prob * (scores[index, place, 1] - rows[1:2, cols])).astype(BF16))
            total[:, cols] += dot(part(0, slice(low, high)), jnp.concatenate(dscores), TN)

    for_each_slab(valid, 0, places, refs[groups:], body)
    out[...] = (total[...] * SCALE).T.astype(BF16)


def query_side(valid, window, kept, rows):
    tokens, dim = window[0][0].shape[1:]
    arrays, places = arrays_of(window)
    return vmem_call(
        functools.partial(query_kernel, places, len(kept)), "query_side", 1, len(window),
        [jax.ShapeDtypeStruct((tokens, dim), BF16)], [pltpu.VMEM((dim, tokens), F32)], valid, rows, *kept, *arrays,
    )[0]


def key_kernel(first, places, finish, valid, kv, rows, *refs):
    totals = refs[-1]
    tokens = kv.shape[1]
    if first == 0:
        totals[...] = jnp.zeros_like(totals)
    else:
        totals[...] = refs[0][...]
        refs = refs[1:]

    def body(number, part):
        for tile in range(tokens // TILE_TOKENS):
            cols = slice(tile * TILE_TOKENS, (tile + 1) * TILE_TOKENS)
            low, high = near(tile, tokens)
            queries = part(0, slice(low, high))
            grads = part(1, slice(low, high))
            scores = dot(kv[0, cols], queries, NT)
            attn_prob = jnp.exp2(scores * SCALE2 - rows[number, 0:1, low:high])
            grad_prob = dot(kv[1, cols], grads, NT)
            dscore = (attn_prob * (grad_prob - rows[number, 1:2, low:high])).astype(BF16)
            key_part = (dot(dscore, queries, NN) * SCALE).astype(BF16)
            value_part = dot(attn_prob.astype(BF16), grads, NN).astype(BF16)
            totals[0, cols] += key_part.astype(F32)
            totals[1, cols] += value_part.astype(F32)

    for_each_slab(valid, first, places, refs, body)
    if finish:
        refs[-3][...] = totals[0].astype(BF16)
        refs[-2][...] = totals[1].astype(BF16)


def key_side(valid, first, kv, window, rows, start, finish):
    tokens, dim = kv.shape[1:]
    arrays, places = arrays_of(window)
    totals = (2, tokens, dim)
    outs = [jax.ShapeDtypeStruct((tokens, dim), BF16)] * 2 if finish else [jax.ShapeDtypeStruct(totals, F32)]
    return vmem_call(
        functools.partial(key_kernel, first, places, finish), "key_side", 4, len(window),
        outs, [pltpu.VMEM(totals, F32)] if finish else [], valid, kv, rows,
        *([] if first == 0 else [start]), *arrays,
    )


def swap_mate(value):
    count = lax.axis_size("tm")
    return lax.ppermute(value, "tm", [(source, source ^ 1) for source in range(count)])


def swap_cross(value):
    count = lax.axis_size("tm")
    return lax.ppermute(value, "tm", [(s, cross_of(s)) for s in range(count) if has_cross(s % ROW_TILES)])


def cross_of(index):
    return index + 1 if index % CHIP_ROWS == CHIP_ROWS - 1 else index - 1


def has_cross(row):
    return 0 <= cross_of(row) < ROW_TILES


def frame_step(frame, phase):
    return 1 - 2 * ((frame + phase) % 2)


def swap_frames(value, phase, cross_only=False):
    count = lax.axis_size("tm")
    pairs = [(s, s + frame_step(s // ROW_TILES, phase) * ROW_TILES) for s in range(count)]
    pairs = [pair for pair in pairs if 0 <= pair[1] < count]
    if cross_only:
        pairs = [pair for pair in pairs if has_cross(pair[0] % ROW_TILES)]
    return lax.ppermute(value, "tm", pairs)


def per_device(queries, key_codes, value_codes, key_scales, value_scales, scale_slot, grad_out):
    index = lax.axis_index("tm")
    frames = lax.axis_size("tm") // ROW_TILES
    frame = index // ROW_TILES
    row = index % ROW_TILES
    cross = functools.reduce(lax.bitwise_or, [row == r for r in range(ROW_TILES) if has_cross(r)]).astype(jnp.int32)
    others = [frame + frame_step(frame, phase) for phase in range(2)]
    frame_a, frame_b = [((other >= 0) & (other < frames)).astype(jnp.int32) for other in others]
    one = jnp.ones((), jnp.int32)
    valid = jnp.stack([one, one, cross, frame_a, frame_b, cross * frame_a, cross * frame_b, frame_a, frame_b])

    kv, qg = prepare(queries, key_codes, value_codes, key_scales, value_scales, scale_slot, grad_out)
    kv_a = swap_frames(kv, 0)
    kv_b = swap_frames(kv, 1)
    kv_cross = swap_cross(kv)
    kv_mate = swap_mate(kv)
    qg_sent, kv_cross = lax.optimization_barrier((qg, kv_cross))
    qg_cross = swap_cross(qg_sent)
    kv_cross_a = swap_frames(kv_cross, 0, True)
    kv_cross_b = swap_frames(kv_cross, 1, True)
    kv_mate_a = swap_mate(kv_a)
    kv_mate_b = swap_mate(kv_b)

    kv_near = [(kv, 0), (kv_mate, 0)]
    kv_next = [(kv_cross, 0), (kv_a, 0), (kv_b, 0)]
    kv_last = [(kv_cross_a, 0), (kv_cross_b, 0), (kv_mate_a, 0), (kv_mate_b, 0)]
    running, kept_near = stats(valid, 0, qg, kv_near, None, False)

    running, kept_next = stats(valid, 2, qg, kv_next, running, False)
    qg_cross, running = lax.optimization_barrier((qg_cross, running))
    qg_pair = jnp.concatenate([qg, qg_cross])
    qg_a = swap_frames(qg_pair, 0)
    qg_b = swap_frames(qg_pair, 1)
    qg_mate = swap_mate(qg)
    qg_mate_a = swap_mate(qg_a)
    qg_mate_b = swap_mate(qg_b)

    rows, kept_last = stats(valid, 5, qg, kv_last, running, True)

    trio = jnp.stack([rows, swap_mate(rows), swap_cross(rows)])
    query_grad = query_side(valid, kv_near + kv_next + kv_last, [kept_near, kept_next, kept_last], rows)
    trio, query_grad = lax.optimization_barrier((trio, query_grad))
    trio_a = swap_frames(trio, 0)
    trio_b = swap_frames(trio, 1)

    qg_near = [(qg, 0), (qg_mate, 0), (qg_cross, 0)]
    qg_next = [(qg_a, 0), (qg_b, 0), (qg_a, 2), (qg_b, 2)]
    qg_last = [(qg_mate_a, 0), (qg_mate_b, 0)]
    rows_next = jnp.stack([trio_a[0], trio_b[0], trio_a[2], trio_b[2]])
    rows_last = jnp.stack([trio_a[1], trio_b[1]])
    (totals,) = key_side(valid, 0, kv, qg_near, trio, None, False)
    (totals,) = key_side(valid, 3, kv, qg_next, rows_next, totals, False)
    key_grad, value_grad = key_side(valid, 7, kv, qg_last, rows_last, totals, True)
    return query_grad, key_grad, value_grad


def solution(mesh):
    whole_axis = ("grp", "tm")
    flat = P(whole_axis)
    split = P(whole_axis, None)
    return jax.shard_map(
        per_device,
        mesh=mesh,
        in_specs=(split, split, split, flat, flat, split, split),
        out_specs=(split, split, split),
        check_vma=False,
    )
```

```python
import functools
import math

import jax
import jax.numpy as jnp
from jax import lax
from jax.experimental import pallas as pl
from jax.experimental.pallas import tpu as pltpu
from jax.sharding import PartitionSpec as P

HEAD_DIM = 128
TILE_TOKENS = 256
ROW_TILES = 4
CHIP_ROWS = 2

SCALE = HEAD_DIM ** (-0.5)
SCALE2 = SCALE * math.log2(math.e)
BIG_NEGATIVE = -1e30
STATS_KEYS = 128
VMEM_LIMIT = 8 * 2**20

F32 = jnp.float32
BF16 = jnp.bfloat16
NT = (((1,), (1,)), ((), ()))
TN = (((0,), (0,)), ((), ()))
NN = (((1,), (0,)), ((), ()))


def dot(left, right, dims):
    return lax.dot_general(left, right, dims, preferred_element_type=F32)


def near(tile, tokens):
    return max(0, tile - 1) * TILE_TOKENS, min(tokens, (tile + 2) * TILE_TOKENS)


def params():
    return pltpu.CompilerParams(vmem_limit_bytes=VMEM_LIMIT)


def cost(products, slabs, tokens, dim):
    pairs = slabs * tokens * tokens
    return pl.CostEstimate(flops=products * pairs * dim, bytes_accessed=slabs * tokens * dim, transcendentals=0)


def prepare(queries, key_codes, value_codes, key_scales, value_scales, scale_slot, grad_out):
    tokens, dim = queries.shape
    blocks = scale_slot.shape[1]
    picker = scale_slot[0][:, None] == jnp.arange(blocks, dtype=jnp.int32)[None, :]

    def scaled(codes, scales):
        picked = jnp.sum(jnp.where(picker, scales[None, :], 0.0), axis=1)
        blocked = codes.astype(F32).reshape(blocks, tokens // blocks, dim)
        return (blocked * picked[:, None, None]).astype(BF16).reshape(tokens, dim)

    kv = jnp.stack([scaled(key_codes, key_scales), scaled(value_codes, value_scales)])
    return kv, jnp.stack([queries, grad_out])


def vmem_call(kernel, name, products, slabs, outs, scratch, *operands):
    tokens, dim = operands[-1].shape[1:]
    vmem = pl.BlockSpec(memory_space=pltpu.VMEM)
    return pl.pallas_call(
        kernel,
        in_specs=[pl.BlockSpec(memory_space=pltpu.SMEM)] + [vmem] * (len(operands) - 1),
        out_specs=[vmem] * len(outs),
        out_shape=outs,
        scratch_shapes=scratch,
        cost_estimate=cost(products, slabs, tokens, dim),
        compiler_params=params(),
        name=name,
    )(*operands)


def arrays_of(window):
    arrays = []
    for array, _ in window:
        if not any(array is other for other in arrays):
            arrays.append(array)
    places = [([array is other for other in arrays].index(True), offset) for array, offset in window]
    return arrays, places


def for_each_slab(valid, first, places, refs, body):
    for number, (place, offset) in enumerate(places):

        @pl.when(valid[first + number] > 0)
        def _(ref=refs[place], offset=offset, number=number):
            body(number, lambda part, rows: ref[offset + part, rows])


def tile_pairs(tokens):
    tiles = tokens // TILE_TOKENS
    return [(tile, key) for tile in range(tiles) for key in range(max(0, tile - 1), min(tiles, tile + 2))]


def stats_kernel(first, places, finish, valid, qg, *refs):
    tokens = qg.shape[1]
    running, kept = refs[-1], refs[-2]
    if first == 0:
        running[0] = jnp.full(running.shape[1:], BIG_NEGATIVE, F32)
        running[1:] = jnp.zeros((2,) + running.shape[1:], F32)
    else:
        running[...] = refs[0][...]
        refs = refs[1:]
    shape = (STATS_KEYS // 8, 8, TILE_TOKENS)

    def body(number, part):
        for tile in range(tokens // TILE_TOKENS):
            cols = slice(tile * TILE_TOKENS, (tile + 1) * TILE_TOKENS)
            top, total, weighted = running[0, :, cols], running[1, :, cols], running[2, :, cols]
            for place, pair in enumerate(tile_pairs(tokens)):
                if pair[0] != tile:
                    continue
                for key in range(0, TILE_TOKENS, STATS_KEYS):
                    inner = slice(key, key + STATS_KEYS)
                    keys = slice(pair[1] * TILE_TOKENS + key, pair[1] * TILE_TOKENS + key + STATS_KEYS)
                    scores = dot(part(0, keys), qg[0, cols], NT) * SCALE2
                    grad_prob = dot(part(1, keys), qg[1, cols], NT)
                    kept[number, place, 0, inner] = scores
                    kept[number, place, 1, inner] = grad_prob
                    scores = scores.reshape(shape)
                    new_top = jnp.maximum(top, jnp.max(scores, axis=0))
                    unscaled = jnp.exp2(scores - new_top[None])
                    rescale = jnp.exp2(top - new_top)
                    top = new_top
                    total = total * rescale + jnp.sum(unscaled, axis=0)
                    weighted = weighted * rescale + jnp.sum(unscaled * grad_prob.reshape(shape), axis=0)
            running[0, :, cols], running[1, :, cols], running[2, :, cols] = top, total, weighted

    for_each_slab(valid, first, places, refs, body)
    if finish:
        final = refs[-3]
        top = running[0]
        row_top = jnp.max(top, axis=0, keepdims=True)
        rescale = jnp.exp2(top - row_top)
        total = jnp.sum(running[1] * rescale, axis=0, keepdims=True)
        weighted = jnp.sum(running[2] * rescale, axis=0, keepdims=True)
        final[0:1] = row_top + jnp.log2(total)
        final[1:2] = weighted / total


def stats(valid, first, qg, window, start, finish):
    tokens = qg.shape[1]
    arrays, places = arrays_of(window)
    running = (3, 8, tokens)
    kept = jax.ShapeDtypeStruct((len(window), len(tile_pairs(tokens)), 2, TILE_TOKENS, TILE_TOKENS), F32)
    result = jax.ShapeDtypeStruct((2, tokens) if finish else running, F32)
    outs = vmem_call(
        functools.partial(stats_kernel, first, places, finish), "row_stats", 2, len(window),
        [result, kept] if finish else [kept, result], [pltpu.VMEM(running, F32)] if finish else [],
        valid, qg, *([] if first == 0 else [start]), *arrays,
    )
    return outs if finish else outs[::-1]


def query_kernel(places, groups, valid, rows, *refs):
    out, total = refs[-2:]
    tokens = rows.shape[1]
    total[...] = jnp.zeros_like(total)
    kept = [(ref, number) for ref in refs[:groups] for number in range(ref.shape[0])]

    def body(number, part):
        scores, index = kept[number]
        for tile in range(tokens // TILE_TOKENS):
            cols = slice(tile * TILE_TOKENS, (tile + 1) * TILE_TOKENS)
            low, high = near(tile, tokens)
            dscores = []
            for place, pair in enumerate(tile_pairs(tokens)):
                if pair[0] == tile:
                    attn_prob = jnp.exp2(scores[index, place, 0] - rows[0:1, cols])
                    dscores.append((attn_prob * (scores[index, place, 1] - rows[1:2, cols])).astype(BF16))
            total[:, cols] += dot(part(0, slice(low, high)), jnp.concatenate(dscores), TN)

    for_each_slab(valid, 0, places, refs[groups:], body)
    out[...] = (total[...] * SCALE).T.astype(BF16)


def query_side(valid, window, kept, rows):
    tokens, dim = window[0][0].shape[1:]
    arrays, places = arrays_of(window)
    return vmem_call(
        functools.partial(query_kernel, places, len(kept)), "query_side", 1, len(window),
        [jax.ShapeDtypeStruct((tokens, dim), BF16)], [pltpu.VMEM((dim, tokens), F32)], valid, rows, *kept, *arrays,
    )[0]


def key_kernel(first, places, finish, valid, kv, rows, *refs):
    totals = refs[-1]
    tokens = kv.shape[1]
    if first == 0:
        totals[...] = jnp.zeros_like(totals)
    else:
        totals[...] = refs[0][...]
        refs = refs[1:]

    def body(number, part):
        tiles = tokens // TILE_TOKENS

        def ends(tile):
            return slice(tile * TILE_TOKENS, (tile + 1) * TILE_TOKENS), slice(*near(tile, tokens))

        def front(tile):
            cols, window = ends(tile)
            return dot(kv[0, cols], part(0, window), NT), dot(kv[1, cols], part(1, window), NT)

        def middle(tile, scores, grad_prob):
            window = ends(tile)[1]
            attn_prob = jnp.exp2(scores * SCALE2 - rows[number, 0:1, window])
            dscore = (attn_prob * (grad_prob - rows[number, 1:2, window])).astype(BF16)
            return dscore, attn_prob.astype(BF16)

        def back(tile, dscore, prob_low):
            cols, window = ends(tile)
            key_part = (dot(dscore, part(0, window), NN) * SCALE).astype(BF16)
            value_part = dot(prob_low, part(1, window), NN).astype(BF16)
            totals[0, cols] += key_part.astype(F32)
            totals[1, cols] += value_part.astype(F32)

        ahead, behind = front(0), None
        for tile in range(tiles):
            now = middle(tile, *ahead)
            if tile + 1 < tiles:
                ahead = front(tile + 1)
            if behind is not None:
                back(tile - 1, *behind)
            behind = now
        back(tiles - 1, *behind)

    for_each_slab(valid, first, places, refs, body)
    if finish:
        refs[-3][...] = totals[0].astype(BF16)
        refs[-2][...] = totals[1].astype(BF16)


def key_side(valid, first, kv, window, rows, start, finish):
    tokens, dim = kv.shape[1:]
    arrays, places = arrays_of(window)
    totals = (2, tokens, dim)
    outs = [jax.ShapeDtypeStruct((tokens, dim), BF16)] * 2 if finish else [jax.ShapeDtypeStruct(totals, F32)]
    return vmem_call(
        functools.partial(key_kernel, first, places, finish), "key_side", 4, len(window),
        outs, [pltpu.VMEM(totals, F32)] if finish else [], valid, kv, rows,
        *([] if first == 0 else [start]), *arrays,
    )


def swap_mate(value):
    count = lax.axis_size("tm")
    return lax.ppermute(value, "tm", [(source, source ^ 1) for source in range(count)])


def swap_cross(value):
    count = lax.axis_size("tm")
    return lax.ppermute(value, "tm", [(s, cross_of(s)) for s in range(count) if has_cross(s % ROW_TILES)])


def cross_of(index):
    return index + 1 if index % CHIP_ROWS == CHIP_ROWS - 1 else index - 1


def has_cross(row):
    return 0 <= cross_of(row) < ROW_TILES


def frame_step(frame, phase):
    return 1 - 2 * ((frame + phase) % 2)


def swap_frames(value, phase, cross_only=False):
    count = lax.axis_size("tm")
    pairs = [(s, s + frame_step(s // ROW_TILES, phase) * ROW_TILES) for s in range(count)]
    pairs = [pair for pair in pairs if 0 <= pair[1] < count]
    if cross_only:
        pairs = [pair for pair in pairs if has_cross(pair[0] % ROW_TILES)]
    return lax.ppermute(value, "tm", pairs)


def per_device(queries, key_codes, value_codes, key_scales, value_scales, scale_slot, grad_out):
    index = lax.axis_index("tm")
    frames = lax.axis_size("tm") // ROW_TILES
    frame = index // ROW_TILES
    row = index % ROW_TILES
    cross = functools.reduce(lax.bitwise_or, [row == r for r in range(ROW_TILES) if has_cross(r)]).astype(jnp.int32)
    others = [frame + frame_step(frame, phase) for phase in range(2)]
    frame_a, frame_b = [((other >= 0) & (other < frames)).astype(jnp.int32) for other in others]
    one = jnp.ones((), jnp.int32)
    valid = jnp.stack([one, one, cross, frame_a, frame_b, cross * frame_a, cross * frame_b, frame_a, frame_b])

    kv, qg = prepare(queries, key_codes, value_codes, key_scales, value_scales, scale_slot, grad_out)
    kv_a = swap_frames(kv, 0)
    kv_b = swap_frames(kv, 1)
    kv_cross = swap_cross(kv)
    kv_mate = swap_mate(kv)
    qg_sent, kv_cross = lax.optimization_barrier((qg, kv_cross))
    qg_cross = swap_cross(qg_sent)
    kv_cross_a = swap_frames(kv_cross, 0, True)
    kv_cross_b = swap_frames(kv_cross, 1, True)
    kv_mate_a = swap_mate(kv_a)
    kv_mate_b = swap_mate(kv_b)

    kv_near = [(kv, 0), (kv_mate, 0)]
    kv_next = [(kv_cross, 0), (kv_a, 0), (kv_b, 0)]
    kv_last = [(kv_cross_a, 0), (kv_cross_b, 0), (kv_mate_a, 0), (kv_mate_b, 0)]
    running, kept_near = stats(valid, 0, qg, kv_near, None, False)

    running, kept_next = stats(valid, 2, qg, kv_next, running, False)
    qg_cross, running = lax.optimization_barrier((qg_cross, running))
    qg_pair = jnp.concatenate([qg, qg_cross])
    qg_a = swap_frames(qg_pair, 0)
    qg_b = swap_frames(qg_pair, 1)
    qg_mate = swap_mate(qg)
    qg_mate_a = swap_mate(qg_a)
    qg_mate_b = swap_mate(qg_b)

    rows, kept_last = stats(valid, 5, qg, kv_last, running, True)

    trio = jnp.stack([rows, swap_mate(rows), swap_cross(rows)])
    query_grad = query_side(valid, kv_near + kv_next + kv_last, [kept_near, kept_next, kept_last], rows)
    trio, query_grad = lax.optimization_barrier((trio, query_grad))
    trio_a = swap_frames(trio, 0)
    trio_b = swap_frames(trio, 1)

    qg_near = [(qg, 0), (qg_mate, 0), (qg_cross, 0)]
    qg_next = [(qg_a, 0), (qg_b, 0), (qg_a, 2), (qg_b, 2)]
    qg_last = [(qg_mate_a, 0), (qg_mate_b, 0)]
    rows_next = jnp.stack([trio_a[0], trio_b[0], trio_a[2], trio_b[2]])
    rows_last = jnp.stack([trio_a[1], trio_b[1]])
    (totals,) = key_side(valid, 0, kv, qg_near, trio, None, False)
    (totals,) = key_side(valid, 3, kv, qg_next, rows_next, totals, False)
    key_grad, value_grad = key_side(valid, 7, kv, qg_last, rows_last, totals, True)
    return query_grad, key_grad, value_grad


def solution(mesh):
    whole_axis = ("grp", "tm")
    flat = P(whole_axis)
    split = P(whole_axis, None)
    return jax.shard_map(
        per_device,
        mesh=mesh,
        in_specs=(split, split, split, flat, flat, split, split),
        out_specs=(split, split, split),
        check_vma=False,
    )
```

```python
import functools
import math

import jax
import jax.numpy as jnp
from jax import lax
from jax.experimental import pallas as pl
from jax.experimental.pallas import tpu as pltpu
from jax.sharding import PartitionSpec as P

HEAD_DIM = 128
TILE_TOKENS = 256
ROW_TILES = 4
CHIP_ROWS = 2

SCALE = HEAD_DIM ** (-0.5)
SCALE2 = SCALE * math.log2(math.e)
BIG_NEGATIVE = -1e30
STATS_KEYS = 128
VMEM_LIMIT = 8 * 2**20

F32 = jnp.float32
BF16 = jnp.bfloat16
NT = (((1,), (1,)), ((), ()))
TN = (((0,), (0,)), ((), ()))
NN = (((1,), (0,)), ((), ()))


def dot(left, right, dims):
    return lax.dot_general(left, right, dims, preferred_element_type=F32)


def near(tile, tokens):
    return max(0, tile - 1) * TILE_TOKENS, min(tokens, (tile + 2) * TILE_TOKENS)


def params():
    return pltpu.CompilerParams(vmem_limit_bytes=VMEM_LIMIT)


def cost(products, slabs, tokens, dim):
    pairs = slabs * tokens * tokens
    return pl.CostEstimate(flops=products * pairs * dim, bytes_accessed=slabs * tokens * dim, transcendentals=0)


def prepare(queries, key_codes, value_codes, key_scales, value_scales, scale_slot, grad_out):
    tokens, dim = queries.shape
    blocks = scale_slot.shape[1]
    picker = scale_slot[0][:, None] == jnp.arange(blocks, dtype=jnp.int32)[None, :]

    def scaled(codes, scales):
        picked = jnp.sum(jnp.where(picker, scales[None, :], 0.0), axis=1)
        blocked = codes.astype(F32).reshape(blocks, tokens // blocks, dim)
        return (blocked * picked[:, None, None]).astype(BF16).reshape(tokens, dim)

    kv = jnp.stack([scaled(key_codes, key_scales), scaled(value_codes, value_scales)])
    return kv, jnp.stack([queries, grad_out])


def vmem_call(kernel, name, products, slabs, outs, scratch, *operands):
    tokens, dim = operands[-1].shape[1:]
    vmem = pl.BlockSpec(memory_space=pltpu.VMEM)
    return pl.pallas_call(
        kernel,
        in_specs=[pl.BlockSpec(memory_space=pltpu.SMEM)] + [vmem] * (len(operands) - 1),
        out_specs=[vmem] * len(outs),
        out_shape=outs,
        scratch_shapes=scratch,
        cost_estimate=cost(products, slabs, tokens, dim),
        compiler_params=params(),
        name=name,
    )(*operands)


def arrays_of(window):
    arrays = []
    for array, _ in window:
        if not any(array is other for other in arrays):
            arrays.append(array)
    places = [([array is other for other in arrays].index(True), offset) for array, offset in window]
    return arrays, places


def for_each_slab(valid, first, places, refs, body):
    for number, (place, offset) in enumerate(places):

        @pl.when(valid[first + number] > 0)
        def _(ref=refs[place], offset=offset, number=number):
            body(number, lambda part, rows: ref[offset + part, rows])


def tile_pairs(tokens):
    tiles = tokens // TILE_TOKENS
    return [(tile, key) for tile in range(tiles) for key in range(max(0, tile - 1), min(tiles, tile + 2))]


def stats_kernel(first, places, finish, valid, qg, *refs):
    tokens = qg.shape[1]
    running, kept = refs[-1], refs[-2]
    if first == 0:
        running[0] = jnp.full(running.shape[1:], BIG_NEGATIVE, F32)
        running[1:] = jnp.zeros((2,) + running.shape[1:], F32)
    else:
        running[...] = refs[0][...]
        refs = refs[1:]
    shape = (STATS_KEYS // 8, 8, TILE_TOKENS)

    def body(number, part):
        for tile in range(tokens // TILE_TOKENS):
            cols = slice(tile * TILE_TOKENS, (tile + 1) * TILE_TOKENS)
            top, total, weighted = running[0, :, cols], running[1, :, cols], running[2, :, cols]
            for place, pair in enumerate(tile_pairs(tokens)):
                if pair[0] != tile:
                    continue
                for key in range(0, TILE_TOKENS, STATS_KEYS):
                    inner = slice(key, key + STATS_KEYS)
                    keys = slice(pair[1] * TILE_TOKENS + key, pair[1] * TILE_TOKENS + key + STATS_KEYS)
                    scores = dot(part(0, keys), qg[0, cols], NT) * SCALE2
                    grad_prob = dot(part(1, keys), qg[1, cols], NT)
                    kept[number, place, 0, inner] = scores
                    kept[number, place, 1, inner] = grad_prob
                    scores = scores.reshape(shape)
                    new_top = jnp.maximum(top, jnp.max(scores, axis=0))
                    unscaled = jnp.exp2(scores - new_top[None])
                    rescale = jnp.exp2(top - new_top)
                    top = new_top
                    total = total * rescale + jnp.sum(unscaled, axis=0)
                    weighted = weighted * rescale + jnp.sum(unscaled * grad_prob.reshape(shape), axis=0)
            running[0, :, cols], running[1, :, cols], running[2, :, cols] = top, total, weighted

    for_each_slab(valid, first, places, refs, body)
    if finish:
        final = refs[-3]
        top = running[0]
        row_top = jnp.max(top, axis=0, keepdims=True)
        rescale = jnp.exp2(top - row_top)
        total = jnp.sum(running[1] * rescale, axis=0, keepdims=True)
        weighted = jnp.sum(running[2] * rescale, axis=0, keepdims=True)
        final[0:1] = row_top + jnp.log2(total)
        final[1:2] = weighted / total


def stats(valid, first, qg, window, start, finish):
    tokens = qg.shape[1]
    arrays, places = arrays_of(window)
    running = (3, 8, tokens)
    kept = jax.ShapeDtypeStruct((len(window), len(tile_pairs(tokens)), 2, TILE_TOKENS, TILE_TOKENS), F32)
    result = jax.ShapeDtypeStruct((2, tokens) if finish else running, F32)
    outs = vmem_call(
        functools.partial(stats_kernel, first, places, finish), "row_stats", 2, len(window),
        [result, kept] if finish else [kept, result], [pltpu.VMEM(running, F32)] if finish else [],
        valid, qg, *([] if first == 0 else [start]), *arrays,
    )
    return outs if finish else outs[::-1]


def query_kernel(places, groups, valid, rows, *refs):
    out, total = refs[-2:]
    tokens = rows.shape[1]
    total[...] = jnp.zeros_like(total)
    kept = [(ref, number) for ref in refs[:groups] for number in range(ref.shape[0])]

    def body(number, part):
        scores, index = kept[number]
        for tile in range(tokens // TILE_TOKENS):
            cols = slice(tile * TILE_TOKENS, (tile + 1) * TILE_TOKENS)
            low, high = near(tile, tokens)
            dscores = []
            for place, pair in enumerate(tile_pairs(tokens)):
                if pair[0] == tile:
                    attn_prob = jnp.exp2(scores[index, place, 0] - rows[0:1, cols])
                    dscores.append((attn_prob * (scores[index, place, 1] - rows[1:2, cols])).astype(BF16))
            total[:, cols] += dot(part(0, slice(low, high)), jnp.concatenate(dscores), TN)

    for_each_slab(valid, 0, places, refs[groups:], body)
    out[...] = (total[...] * SCALE).T.astype(BF16)


def query_side(valid, window, kept, rows):
    tokens, dim = window[0][0].shape[1:]
    arrays, places = arrays_of(window)
    return vmem_call(
        functools.partial(query_kernel, places, len(kept)), "query_side", 1, len(window),
        [jax.ShapeDtypeStruct((tokens, dim), BF16)], [pltpu.VMEM((dim, tokens), F32)], valid, rows, *kept, *arrays,
    )[0]


def key_kernel(first, places, finish, valid, kv, rows, *refs):
    totals = refs[-1]
    tokens = kv.shape[1]
    if first == 0:
        totals[...] = jnp.zeros_like(totals)
    else:
        totals[...] = refs[0][...]
        refs = refs[1:]

    def body(number, part):
        tiles = tokens // TILE_TOKENS

        def ends(tile):
            return slice(tile * TILE_TOKENS, (tile + 1) * TILE_TOKENS), slice(*near(tile, tokens))

        def front(tile):
            cols, window = ends(tile)
            return dot(kv[0, cols], part(0, window), NT), dot(kv[1, cols], part(1, window), NT)

        def middle(tile, scores, grad_prob):
            window = ends(tile)[1]
            attn_prob = jnp.exp2(scores * SCALE2 - rows[number, 0:1, window])
            dscore = (attn_prob * (grad_prob - rows[number, 1:2, window])).astype(BF16)
            return dscore, attn_prob.astype(BF16)

        def back(tile, dscore, prob_low):
            cols, window = ends(tile)
            key_part = (dot(dscore, part(0, window), NN) * SCALE).astype(BF16)
            value_part = dot(prob_low, part(1, window), NN).astype(BF16)
            totals[0, cols] += key_part.astype(F32)
            totals[1, cols] += value_part.astype(F32)

        ahead, behind = front(0), None
        for tile in range(tiles):
            now = middle(tile, *ahead)
            if tile + 1 < tiles:
                ahead = front(tile + 1)
            if behind is not None:
                back(tile - 1, *behind)
            behind = now
        back(tiles - 1, *behind)

    for_each_slab(valid, first, places, refs, body)
    if finish:
        refs[-3][...] = totals[0].astype(BF16)
        refs[-2][...] = totals[1].astype(BF16)


def key_side(valid, first, kv, window, rows, start, finish):
    tokens, dim = kv.shape[1:]
    arrays, places = arrays_of(window)
    totals = (2, tokens, dim)
    outs = [jax.ShapeDtypeStruct((tokens, dim), BF16)] * 2 if finish else [jax.ShapeDtypeStruct(totals, F32)]
    return vmem_call(
        functools.partial(key_kernel, first, places, finish), "key_side", 4, len(window),
        outs, [pltpu.VMEM(totals, F32)] if finish else [], valid, kv, rows,
        *([] if first == 0 else [start]), *arrays,
    )


def swap_mate(value):
    count = lax.axis_size("tm")
    return lax.ppermute(value, "tm", [(source, source ^ 1) for source in range(count)])


def swap_cross(value):
    count = lax.axis_size("tm")
    return lax.ppermute(value, "tm", [(s, cross_of(s)) for s in range(count) if has_cross(s % ROW_TILES)])


def cross_of(index):
    return index + 1 if index % CHIP_ROWS == CHIP_ROWS - 1 else index - 1


def has_cross(row):
    return 0 <= cross_of(row) < ROW_TILES


def frame_step(frame, phase):
    return 1 - 2 * ((frame + phase) % 2)


def swap_frames(value, phase, cross_only=False):
    count = lax.axis_size("tm")
    pairs = [(s, s + frame_step(s // ROW_TILES, phase) * ROW_TILES) for s in range(count)]
    pairs = [pair for pair in pairs if 0 <= pair[1] < count]
    if cross_only:
        pairs = [pair for pair in pairs if has_cross(pair[0] % ROW_TILES)]
    return lax.ppermute(value, "tm", pairs)


def per_device(queries, key_codes, value_codes, key_scales, value_scales, scale_slot, grad_out):
    index = lax.axis_index("tm")
    frames = lax.axis_size("tm") // ROW_TILES
    frame = index // ROW_TILES
    row = index % ROW_TILES
    cross = functools.reduce(lax.bitwise_or, [row == r for r in range(ROW_TILES) if has_cross(r)]).astype(jnp.int32)
    others = [frame + frame_step(frame, phase) for phase in range(2)]
    frame_a, frame_b = [((other >= 0) & (other < frames)).astype(jnp.int32) for other in others]
    one = jnp.ones((), jnp.int32)
    valid = jnp.stack([one, one, cross, frame_a, frame_b, cross * frame_a, cross * frame_b, frame_a, frame_b])

    kv, qg = prepare(queries, key_codes, value_codes, key_scales, value_scales, scale_slot, grad_out)
    kv_a = swap_frames(kv, 0)
    kv_b = swap_frames(kv, 1)
    kv_cross = swap_cross(kv)
    kv_mate = swap_mate(kv)
    qg_sent, kv_cross = lax.optimization_barrier((qg, kv_cross))
    qg_cross = swap_cross(qg_sent)
    kv_cross_a = swap_frames(kv_cross, 0, True)
    kv_cross_b = swap_frames(kv_cross, 1, True)
    kv_mate_a = swap_mate(kv_a)
    kv_mate_b = swap_mate(kv_b)

    kv_near = [(kv, 0), (kv_mate, 0)]
    kv_next = [(kv_cross, 0), (kv_a, 0), (kv_b, 0)]
    kv_third = [(kv_cross_a, 0), (kv_cross_b, 0)]
    kv_last = [(kv_mate_a, 0), (kv_mate_b, 0)]
    running, kept_near = stats(valid, 0, qg, kv_near, None, False)

    running, kept_next = stats(valid, 2, qg, kv_next, running, False)
    qg_cross, running = lax.optimization_barrier((qg_cross, running))
    qg_pair = jnp.concatenate([qg, qg_cross])
    qg_a = swap_frames(qg_pair, 0)
    qg_b = swap_frames(qg_pair, 1)
    qg_mate = swap_mate(qg)
    qg_mate_a = swap_mate(qg_a)
    qg_mate_b = swap_mate(qg_b)

    running, kept_third = stats(valid, 5, qg, kv_third, running, False)
    rows, kept_last = stats(valid, 7, qg, kv_last, running, True)

    trio = jnp.stack([rows, swap_mate(rows), swap_cross(rows)])
    query_grad = query_side(
        valid, kv_near + kv_next + kv_third + kv_last, [kept_near, kept_next, kept_third, kept_last], rows
    )
    trio, query_grad = lax.optimization_barrier((trio, query_grad))
    trio_a = swap_frames(trio, 0)
    trio_b = swap_frames(trio, 1)

    qg_near = [(qg, 0), (qg_mate, 0), (qg_cross, 0)]
    qg_next = [(qg_a, 0), (qg_b, 0), (qg_a, 2), (qg_b, 2)]
    qg_last = [(qg_mate_a, 0), (qg_mate_b, 0)]
    rows_next = jnp.stack([trio_a[0], trio_b[0], trio_a[2], trio_b[2]])
    rows_last = jnp.stack([trio_a[1], trio_b[1]])
    (totals,) = key_side(valid, 0, kv, qg_near, trio, None, False)
    (totals,) = key_side(valid, 3, kv, qg_next, rows_next, totals, False)
    key_grad, value_grad = key_side(valid, 7, kv, qg_last, rows_last, totals, True)
    return query_grad, key_grad, value_grad


def solution(mesh):
    whole_axis = ("grp", "tm")
    flat = P(whole_axis)
    split = P(whole_axis, None)
    return jax.shard_map(
        per_device,
        mesh=mesh,
        in_specs=(split, split, split, flat, flat, split, split),
        out_specs=(split, split, split),
        check_vma=False,
    )
```
